32 devices in a mesh: groups: 2 (over y), lib: 4 (over z), tmpl: 2 (over x), sub: 2 (over core).
Axes of the slice: x: 2, y: 2, z: 4, core: 2. Of those that a mesh axis runs over, the one named last changes fastest.
Arguments:
- coords: float32 [512, 3, 128], P(('groups', 'lib', 'tmpl')), parts along dimension 0, may hold values from -5 to 5
- atom_type: int32 [512, 128], P(('groups', 'lib', 'tmpl')), parts along dimension 0, may hold values from 0 to 15
- channel: int32 [512, 128], P(('groups', 'lib', 'tmpl')), parts along dimension 0, may hold values from 0 to 2
- charge: float32 [512, 128], P(('groups', 'lib', 'tmpl')), parts along dimension 0, may hold values from -3 to 3
- pair_owner: int32 [512, 4], P(('groups', 'lib', 'tmpl')), parts along dimension 0, may hold values from 0 to 7, all different within a row; in each aligned block of 32 rows (0 to 31, 32 to 63, ...) at most 32 rows name the same one
- pair_slot: int32 [512, 4], P(('groups', 'lib', 'tmpl')), parts along dimension 0, may hold values from 0 to 511
- type_table: float32 [16, 2], replicated, may hold values from 0.3 to 3
- widths: float32 [5], replicated, may hold values from 0.3 to 1.2
- tmpl_points: float32 [4096, 3, 256], P(('lib', 'tmpl'), None, 'sub'), may hold values from -5 to 5
- tmpl_weights: bfloat16 [4096, 5, 256], P(('lib', 'tmpl'), None, 'sub'), may hold values from -3 to 3
Outputs:
- scores: float32 [512, 4], P(('groups', 'lib', 'tmpl')), parts along dimension 0
- pose_grad: float32 [512, 12], P(('groups', 'lib', 'tmpl')), parts along dimension 0
- weight_grad: float32 [8192, 5, 256], P(('groups', 'lib', 'tmpl'), None, 'sub'), parts along dimension 0
The draws below stay inside these ranges and needn't reach their ends.
There are 2 independent parts, one for each index of `groups`. The reference program is written for one: setup_inputs(seed, part) draws one part's arguments, and reference() takes and returns one part's arrays. A program takes and returns all parts, laid end to end along the dimension named above; an argument that names none is the same for every part. Nothing has to cross between parts.
Inputs may be any that keep to these rules, and one draw needn't show every extreme that they name: `pair_owner`: each row names 4 different owners; among the 32 rows of one device (aligned blocks) no owner is named more than 32 times, a bound that some block reaches.
All inputs are finite; a program needn't handle non-finite values.
Results may differ from the reference program's by a relative error of at most 0.0003.
Values sent between devices are 32-bit elements; how exact they have to be, the bound alone decides.
No kernel may reach another device: no remote copies, remote signals or barrier semaphores. Data moves between devices by JAX's collectives and lax.ppermute only.
A program may use at most 64 MiB of HBM per device.

```python
import math
import jax
import jax.numpy as jnp
import numpy as np
from jax import lax

A = 128
TA = 256
F = 5
NT = 16
TOP = 4
TEMPLATES = 4096
CB = 32
OWNERS = 8
CAP = 32
TMPL_DEV = 512
BLOCKS = 256


def touch_ends(array, stream_key, least, largest):
    longest = array.shape.index(max(array.shape))
    spots = []
    for shift in (0, 1):
        where = [jax.random.randint(jax.random.fold_in(stream_key, axis), (), 0, length) for axis, length in enumerate(array.shape)]
        where[longest] = (where[longest] + shift) % array.shape[longest]
        spots.append(tuple(where))
    return array.at[spots[0]].set(least).at[spots[1]].set(largest)


def shard_levels(stream_key, dims, shards, low, largest):
    gain = 1.0
    for position, parts in shards:
        heights = jax.random.uniform(jax.random.fold_in(jax.random.fold_in(stream_key, 6), position), (parts,), jnp.float32, low / len(shards), largest / len(shards))
        gain = gain * jnp.repeat(jnp.exp(heights), dims[position] // parts).reshape((-1,) + (1,) * (len(dims) - 1 - position))
    return gain


def deal_out(stream_key, own, number, rows, amount, top, limit, slope):
    ranking = jax.random.permutation(stream_key, amount)
    crowded, ordinary = portions_of(amount, rows * top, limit, slope, True), portions_of(amount, rows * top, limit, slope, False)
    places = jnp.arange(amount)

    def named(tallies, rotation):
        used = int((tallies > 0).sum())
        fixed = max(1, used // 4)
        moved = fixed + (places - fixed + rotation * (used - fixed)) % max(1, amount - fixed)
        return jnp.zeros((amount,), jnp.int32).at[ranking[jnp.where(places < fixed, places, moved)]].set(jnp.asarray(tallies, jnp.int32))

    tallies = jnp.where(number % 4 == 0, named(crowded, number // 4), named(ordinary, number - number // 4 - 1))
    mixed = jax.random.permutation(jax.random.fold_in(own, 3), amount)
    giver, receiver = mixed[0:amount // 2 * 2:2], mixed[1:amount // 2 * 2:2]
    margin = jnp.minimum(tallies[giver] - 1, limit - tallies[receiver]) // 2
    margin = jnp.where((giver == ranking[0]) | (receiver == ranking[0]) | (tallies[receiver] == 0), 0, jnp.maximum(margin, 0))
    moved = jax.random.randint(jax.random.fold_in(own, 4), (amount // 2,), 0, 1 << 20) % (margin + 1)
    tallies = tallies.at[giver].add(-moved).at[receiver].add(moved)
    members = jnp.searchsorted(jnp.cumsum(tallies), jnp.arange(rows * top), side="right").astype(jnp.int32)
    listing = members.reshape(top, rows).T
    listing = listing[jax.random.permutation(jax.random.fold_in(own, 1), rows)]
    rotation = jax.random.randint(jax.random.fold_in(own, 2), (rows, 1), 0, top)
    return jnp.take_along_axis(listing, (jnp.arange(top)[None, :] + rotation) % top, axis=1)


def portions_of(amount, total, bound, lean, full):
    loads = [(1 << 20) // math.isqrt(standing ** lean) + 1 for standing in range(1, amount + 1)]
    largest = bound if full else min(bound, max(-(-total // amount), total * loads[0] // sum(loads)))
    least = 1 if total - largest >= amount - 1 else 0
    holding, spare = [largest] + [least] * (amount - 1), total - largest - least * (amount - 1)
    while spare > 0:
        free = [i for i in range(1, amount) if holding[i] < largest] or [i for i in range(1, amount) if holding[i] < bound]
        pool, remaining = sum([loads[i] for i in free]), spare
        for i in free:
            extra = min(bound - holding[i], max(1, remaining * loads[i] // pool), spare)
            holding[i] = holding[i] + extra
            spare = spare - extra
    return np.array(holding)


def centred(rng, shape, scale, limit, split=(), kind=jnp.bfloat16):
    array = jax.random.normal(rng, shape, jnp.float32) * scale
    if len(split) > 0:
        array = shard_levels(rng, shape, split, -0.22, 0.18) * array
    return jnp.clip(array, min=-limit, max=limit).astype(kind)


def setup_inputs(seed: int = 0, part: int = 0) -> dict:
    key_of = jax.random.split(jax.random.key(seed), 11)
    part_keys = jax.random.split(jax.random.fold_in(key_of[10], part), 11)
    coords = centred(part_keys[0], (BLOCKS, 3, A), 1.0, 5.0, ((0, 8),), jnp.float32)
    atom_type = touch_ends(jax.random.randint(part_keys[1], (BLOCKS, A), 0, NT), jax.random.fold_in(part_keys[1], 1), 0, NT - 1).astype(jnp.int32)
    channel = touch_ends(jax.random.randint(part_keys[2], (BLOCKS, A), 0, 3), jax.random.fold_in(part_keys[2], 1), 0, 2).astype(jnp.int32)
    charge = centred(part_keys[3], (BLOCKS, A), 0.5, 3.0, ((0, 8),), jnp.float32)
    pair_owner_keys = jax.random.split(jax.random.fold_in(part_keys[4], 1), BLOCKS // CB)
    pair_owner_turns = jax.random.permutation(jax.random.fold_in(part_keys[4], 3), BLOCKS // CB)
    pair_owner = jax.vmap(lambda own, number: deal_out(jax.random.fold_in(part_keys[4], 2), own, number, CB, OWNERS, TOP, CAP, 2))(pair_owner_keys, pair_owner_turns).reshape((BLOCKS, TOP))
    pair_slot = touch_ends(jax.random.randint(part_keys[5], (BLOCKS, TOP), 0, TMPL_DEV), jax.random.fold_in(part_keys[5], 1), 0, TMPL_DEV - 1).astype(jnp.int32)
    type_table = jnp.clip(jnp.exp(jax.random.uniform(key_of[6], (NT, 2), jnp.float32, math.log(0.3), math.log(3.0))), 0.3, 3.0)
    widths = jnp.clip(jnp.exp(jax.random.uniform(key_of[7], (F,), jnp.float32, math.log(0.3), math.log(1.2))), 0.3, 1.2)
    tmpl_points = centred(key_of[8], (TEMPLATES, 3, TA), 1.0, 5.0, ((0, 8), (2, 2)), jnp.float32)
    tmpl_weights = centred(key_of[9], (TEMPLATES, F, TA), 0.5, 3.0, ((0, 8), (2, 2)))
    return dict(coords=coords, atom_type=atom_type, channel=channel, charge=charge, pair_owner=pair_owner, pair_slot=pair_slot, type_table=type_table, widths=widths, tmpl_points=tmpl_points, tmpl_weights=tmpl_weights)


def atom_weights(atom_type, channel, charge, type_table):
    type_ids = jnp.arange(type_table.shape[0], dtype=jnp.int32)
    onehot = (atom_type[:, None, :] == type_ids[None, :, None]).astype(jnp.float32)
    steric = jnp.sum(onehot * type_table[None, :, 0:1], axis=1)
    strength = jnp.sum(onehot * type_table[None, :, 1:2], axis=1)
    channels = jnp.arange(3, dtype=jnp.int32)
    pharm_part = (channel[:, None, :] == channels[None, :, None]).astype(jnp.float32) * strength[:, None, :]
    return jnp.concatenate([steric[:, None, :], charge[:, None, :], pharm_part], axis=1)


def pair_terms(posed_xyz, atom_w, points, values, widths):
    offsets = posed_xyz[:, None, :] - points[:, :, None]
    sq_dist = jnp.sum(offsets * offsets, axis=0)
    kernel = jnp.exp(-widths[:, None, None] * sq_dist[None, :, :])
    crossed = kernel * atom_w[:, None, :]
    fields = crossed * values[:, :, None]
    intersection = jnp.sum(fields)
    scaled = jnp.sum(fields * (-2.0 * widths)[:, None, None], axis=0)
    forces = jnp.sum(scaled[None, :, :] * offsets, axis=1)
    shift_grad = jnp.sum(forces, axis=1)
    linear = jnp.sum(forces[:, None, :] * posed_xyz[None, :, :], axis=2).reshape(9)
    weight_part = jnp.sum(crossed, axis=2)
    return jnp.concatenate([intersection[None], shift_grad, linear]), weight_part


def reference(coords, atom_type, channel, charge, pair_owner, pair_slot, type_table, widths, tmpl_points, tmpl_weights):
    atom_w = atom_weights(atom_type, channel, charge, type_table)
    tmpl_w = tmpl_weights.astype(jnp.float32)
    templates = (pair_owner * TMPL_DEV + pair_slot).astype(jnp.int32)

    def advance(running, element):
        posed_xyz, block_w, tmpl_ids = element

        def single(tmpl_id):
            points = lax.dynamic_index_in_dim(tmpl_points, tmpl_id, 0, keepdims=False)
            values = lax.dynamic_index_in_dim(tmpl_w, tmpl_id, 0, keepdims=False)
            return pair_terms(posed_xyz, block_w, points, values, widths)

        results, weight_part = lax.map(single, tmpl_ids)
        running = running.at[tmpl_ids].add(weight_part)
        return running, results

    initial = jnp.zeros((TEMPLATES, F, TA), jnp.float32)
    weight_grad, results = lax.scan(advance, initial, (coords, atom_w, templates))
    scores = results[:, :, 0]
    pose_grad = jnp.sum(results[:, :, 1:], axis=1)
    return (scores, pose_grad, weight_grad)
```

```python
import functools
import math
import jax
import jax.numpy as jnp
from jax import lax
from jax.experimental import pallas as pl
from jax.experimental.pallas import tpu as pltpu
from jax.sharding import PartitionSpec as P

bf16, f32 = jnp.bfloat16, jnp.float32
LOG2E = math.log2(math.e)
OWN = ("lib", "tmpl")
ROWS = 7
PP = 4


def split3(x):
    h = x.astype(bf16).astype(f32)
    r = x - h
    m = r.astype(bf16).astype(f32)
    return h, m, r - m


def split2(x):
    h = x.astype(bf16)
    return h, (x - h.astype(f32)).astype(bf16)


def body(*refs, blocks, tmpl, parts):
    srcs, refs = refs[:parts], refs[parts:]
    widths_ref, table_ref, pts_ref, wts_ref, wg_ref, res_ref, feats_ref, v_ref, s_ref, tab_ref, idv_ref, ids_ref, sem, idsem = refs[:14]
    bufs = refs[14:]
    half = len(bufs) // 2
    A, B = bufs[:half], bufs[half:]
    copies = []
    if parts == 1:
        copies.append(pltpu.make_async_copy(srcs[0], feats_ref, sem.at[0]))
    else:
        senders, _, rows, _ = srcs[0].shape
        for h in range(parts):
            for o in range(senders):
                to = feats_ref.at[:, pl.ds((o * parts + h) * rows, rows), :]
                copies.append(pltpu.make_async_copy(srcs[h].at[o], to, sem.at[h * senders + o]))
    for c in copies:
        c.start()
    wg_ref[...] = jnp.zeros_like(wg_ref)
    v_ref[...] = wts_ref[...].astype(f32)
    for r in A + B:
        r[...] = jnp.zeros_like(r)
    width = [widths_ref[f] for f in range(5)]
    s0 = -LOG2E * width[0]
    ratio = width[1] / width[0]
    row8 = lax.broadcasted_iota(jnp.int32, (8, 128), 0)
    tab_ref[...] = jnp.zeros_like(tab_ref)
    tab_ref[0:2, 0:16] = table_ref[...]
    tab0 = jnp.broadcast_to(tab_ref[0:1, :], (8, 128))
    tab1 = jnp.broadcast_to(tab_ref[1:2, :], (8, 128))
    scale = [jnp.where(row8 == 0, 1.0, -2.0 * width[f]) for f in range(5)]

    for c in copies:
        c.wait()
    owner = lax.axis_index("lib") * lax.axis_size("tmpl") + lax.axis_index("tmpl")
    near = feats_ref[ROWS - 1] - (owner * tmpl).astype(f32)
    named = (near >= 0.0) & (near < float(tmpl)) & (lax.broadcasted_iota(jnp.int32, near.shape, 1) < 4)
    h, l = split2(jnp.where(named, near + 1.0, 0.0))
    ids = lax.dot_general(jnp.ones((8, 256), bf16), jnp.concatenate([h, l], axis=1), (((1,), (1,)), ((), ())), preferred_element_type=f32)
    idv_ref[...] = ids.astype(jnp.int32) - 1
    copy = pltpu.make_async_copy(idv_ref.at[pl.ds(0, 1)], ids_ref, idsem)
    copy.start()
    copy.wait()

    def slot(b):
        t = ids_ref[0, b]
        return jnp.maximum(t, 0), (t >= 0).astype(f32)

    def stage0(b0, xt_ref, w_ref):
        for u in range(PP // 2):
            cols = []
            for k in range(2):
                b = b0 + 2 * u + k
                _, valid = slot(b)

                def row(k):
                    return jnp.broadcast_to(feats_ref[k, pl.ds(b, 1), :], (8, 128))

                x0, x1, x2 = row(0), row(1), row(2)
                charge = row(3) * valid
                kind = row(4).astype(jnp.int32)
                chan = row(5)
                steric = jnp.take_along_axis(tab0, kind, axis=1) * valid
                strength = jnp.take_along_axis(tab1, kind, axis=1) * valid
                sph = -LOG2E * jnp.where(chan == 0.0, width[2], jnp.where(chan == 1.0, width[3], width[4]))
                x00, x11, x22 = x0 * x0, x1 * x1, x2 * x2
                feat = jnp.where(row8 == 0, x0, jnp.where(row8 == 1, x1, jnp.where(row8 == 2, x2,
                    jnp.where(row8 == 3, x00 + x11 + x22, jnp.where(row8 == 4, 1.0, 0.0)))))
                parts = []
                for sc in (s0, sph):
                    h, m, l = split3(feat * sc)
                    parts.append(jnp.concatenate([h, h, h, m, m, l], axis=0))
                cols.append(jnp.concatenate(parts, axis=1))
                lo8 = jnp.where(row8 == 0, 1.0, jnp.where(row8 == 1, x0, jnp.where(row8 == 2, x1, jnp.where(row8 == 3, x2,
                      jnp.where(row8 == 4, x00, jnp.where(row8 == 5, x0 * x1, jnp.where(row8 == 6, x0 * x2, x11)))))))
                hi8 = jnp.where(row8 == 0, x1 * x2, jnp.where(row8 == 1, x22, jnp.where(row8 == 2, 1.0, 0.0)))
                ws = [steric, charge] + [jnp.where(chan == float(c), strength, 0.0) for c in range(3)]
                hs = [split2(jnp.concatenate([lo8 * w, hi8 * w], axis=0)) for w in ws]
                order = [hs[0][0], hs[0][1], hs[1][0], hs[1][1]] + [z[0] for z in hs[2:]] + [z[1] for z in hs[2:]]
                w_ref[2 * u + k] = jnp.concatenate(order, axis=0)
            xt_ref[u] = jnp.concatenate(cols, axis=0).T.astype(bf16)

    def stage1(b0, xt_ref, a_ref):
        for u in range(PP // 2):
            rhs = []
            for k in range(2):
                t, _ = slot(b0 + 2 * u + k)
                yb = [jnp.broadcast_to(pts_ref[pl.ds(c * tmpl + t, 1), :], (8, 128)) for c in range(3)]
                ysq = yb[0] * yb[0] + yb[1] * yb[1] + yb[2] * yb[2]
                yf = jnp.where(row8 < 3, -2.0 * jnp.where(row8 == 0, yb[0], jnp.where(row8 == 1, yb[1], yb[2])),
                     jnp.where(row8 == 3, 1.0, jnp.where(row8 == 4, ysq, 0.0)))
                h, m, l = split3(yf)
                yk = jnp.concatenate([h, m, l, h, m, h], axis=0).astype(bf16)
                z = jnp.zeros_like(yk)
                rhs.append(jnp.concatenate([yk, z] if k == 0 else [z, yk], axis=1))
            a_ref[u] = jnp.dot(xt_ref[u], jnp.concatenate(rhs, axis=0), preferred_element_type=f32)

    def stage2(a_ref, w_ref, r_ref):
        for u in range(PP // 2):
            for k in range(2):
                js = slice(128 * k, 128 * k + 128)
                lanes = w_ref[2 * u + k]
                def contract(e, rows):
                    eh, el = split2(e)
                    n = rows.shape[0] // 2
                    o = jnp.dot(jnp.concatenate([rows, rows], axis=1), jnp.concatenate([eh, el], axis=0), preferred_element_type=f32)
                    return o[:n] + o[n:]
                a0 = a_ref[u, 0:128, js]
                r_ref[2 * u + k, 0:16] = contract(jnp.exp2(a0), lanes[0:32])
                r_ref[2 * u + k, 16:32] = contract(jnp.exp2(a0 * ratio), lanes[32:64])
                r_ref[2 * u + k, 32:80] = contract(jnp.exp2(a_ref[u, 128:256, js]), lanes[64:160])

    def stage3(b0, r_ref):
        for q in range(PP):
            b = b0 + q
            t, _ = slot(b)
            lo = hi = None
            for f in range(5):
                v = v_ref[pl.ds(f * tmpl + t, 1), :]
                r0 = r_ref[q, 16 * f:16 * f + 8]
                pl_ = r0 * (v * scale[f]); ph_ = r_ref[q, 16 * f + 8:16 * f + 16] * (v * (-2.0 * width[f]))
                lo = pl_ if lo is None else lo + pl_
                hi = ph_ if hi is None else hi + ph_
                dst = pl.ds(f * tmpl + t, 1)
                wg_ref[dst, :] = wg_ref[dst, :] + r0[0:1]
            for n in range(8):
                s_ref[pl.ds(n * blocks + b, 1), :] = lo[n:n + 1]
            for n in range(3):
                s_ref[pl.ds((8 + n) * blocks + b, 1), :] = hi[n:n + 1]
            for c in range(3):
                s_ref[pl.ds((11 + c) * blocks + b, 1), :] = pts_ref[pl.ds(c * tmpl + t, 1), :]

    n = blocks // PP
    def at(i):
        return jnp.clip(i, 0, n - 1) * PP
    def halfstep(i, src, dst):
        xt_s, w1_s, a_s, w2_s, r_s = src
        xt_d, w1_d, a_d, w2_d, r_d = dst
        stage3(at(i - 3), r_s)
        stage2(a_s, w2_s, r_d)
        stage1(at(i - 1), xt_s, a_d)
        w2_d[...] = w1_s[...]
        stage0(at(i), xt_d, w1_d)

    def step(i, _):
        halfstep(2 * i, A, B)
        halfstep(2 * i + 1, B, A)
        return 0
    lax.fori_loop(0, (n + 2) // 2, step, 0)
    stage3((n - 1) * PP, A[-1])

    ones = jnp.ones((8, 256), bf16)
    def col(n):
        return s_ref[n * blocks:(n + 1) * blocks, :]
    def put(n, m):
        h, l = split2(m)
        o = lax.dot_general(ones, jnp.concatenate([h, l], axis=1), (((1,), (1,)), ((), ())), preferred_element_type=f32)
        res_ref[n:n + 1, :] = o[0:1]
    put(0, col(0))
    y = [col(11 + c) for c in range(3)]
    t0 = col(10)
    for c in range(3):
        put(1 + c, col(1 + c) - y[c] * t0)
    idx = {(0, 0): 4, (0, 1): 5, (0, 2): 6, (1, 1): 7, (1, 2): 8, (2, 2): 9}
    for c in range(3):
        for d in range(3):
            put(4 + 3 * c + d, col(idx[min(c, d), max(c, d)]) - y[c] * col(1 + d))
    res_ref[13:16, :] = jnp.zeros((3, res_ref.shape[1]), f32)


def pair_sums(feats, table, widths, pts, wts):
    tmpl = pts.shape[0] // 3
    parts = len(feats)
    if parts == 1:
        blocks, count = feats[0].shape[1], 1
    else:
        blocks, count = parts * feats[0].shape[0] * feats[0].shape[2], parts * feats[0].shape[0]
    any_, vmem, smem = (pl.BlockSpec(memory_space=m) for m in (pl.ANY, pltpu.VMEM, pltpu.SMEM))
    stages = [
        pltpu.VMEM((PP // 2, 256, 96), bf16),
        pltpu.VMEM((PP, 160, 128), bf16),
        pltpu.VMEM((PP // 2, 256, 256), f32),
        pltpu.VMEM((PP, 160, 128), bf16),
        pltpu.VMEM((PP, 80, 128), f32),
    ]
    return pl.pallas_call(
        functools.partial(body, blocks=blocks, tmpl=tmpl, parts=parts),
        out_shape=(jax.ShapeDtypeStruct((5 * tmpl, 128), f32), jax.ShapeDtypeStruct((16, blocks), f32)),
        in_specs=[any_] * parts + [smem, vmem, vmem, vmem],
        out_specs=(vmem, vmem),
        scratch_shapes=[
            pltpu.VMEM((ROWS, blocks, 128), f32),
            pltpu.VMEM((5 * tmpl, 128), f32),
            pltpu.VMEM((14 * blocks, 128), f32),
            pltpu.VMEM((8, 128), f32),
            pltpu.VMEM((8, blocks), jnp.int32),
            pltpu.SMEM((1, blocks), jnp.int32),
            pltpu.SemaphoreType.DMA((count,)),
            pltpu.SemaphoreType.DMA,
        ] + stages + stages,
        compiler_params=pltpu.CompilerParams(vmem_limit_bytes=40 * 1024 * 1024),
        name="gauss",
    )(*feats, widths, table.T, pts, wts)


def local(coords, atom_type, channel, charge, pair_owner, pair_slot, type_table, widths, tmpl_points, tmpl_weights):
    block_count, per_block = pair_owner.shape
    tmpl_count = tmpl_points.shape[0]
    owners = lax.axis_size(OWN)
    pair_count = block_count * per_block
    capacity = max(2, 2 * pair_count // owners)
    pts = tmpl_points.transpose(1, 0, 2).reshape(3 * tmpl_count, 128)
    wts = tmpl_weights.transpose(1, 0, 2).reshape(5 * tmpl_count, 128)
    tids = (pair_owner * tmpl_count + pair_slot).astype(f32)
    atoms = jnp.concatenate(
        [coords.transpose(1, 0, 2), jnp.stack([charge, atom_type.astype(f32), channel.astype(f32)])], axis=0
    )
    if capacity >= block_count:
        tids = jnp.pad(tids, ((0, 0), (0, 128 - per_block)), constant_values=-1.0)
        payload = jnp.concatenate([atoms, tids[None]], axis=0)
        rows = block_count // 2
        sub = lax.axis_index("sub")
        mine = lax.dynamic_slice_in_dim(payload, sub * rows, rows, axis=1)
        sent = jnp.broadcast_to(mine[None], (owners,) + mine.shape)
        first = lax.all_to_all(sent, OWN, split_axis=0, concat_axis=0, tiled=True)
        second = lax.ppermute(first, "sub", [(0, 1), (1, 0)])
        wg, res = pair_sums([first, second], type_table, widths, pts, wts)
        out = res.reshape(16, owners, block_count).transpose(1, 0, 2).reshape(owners, 1, 4, 128)
        out = jnp.broadcast_to(out, (owners, 2, 4, 128)).reshape(owners * 2, 4, 128)
        got = lax.all_to_all(out, OWN + ("sub",), split_axis=0, concat_axis=0, tiled=True)
        got = got.reshape(owners, 2, 16, 2, rows)
        got = (got[:, 0] + got[:, 1, :, ::-1]).reshape(owners, 16, block_count)
        pose_grad = jnp.sum(got[:, 1:13], axis=0).T
        here = (pair_owner[None] == jnp.arange(owners, dtype=jnp.int32)[:, None, None]).astype(f32)
        scores = jnp.sum(here * got[:, 0, :, None], axis=0)
    else:
        owner_ids = pair_owner.reshape(pair_count)
        order = jnp.arange(pair_count, dtype=jnp.int32)
        earlier = (owner_ids[None, :] == owner_ids[:, None]) & (order[None, :] < order[:, None])
        rank = jnp.sum(earlier.astype(jnp.int32), axis=1)
        place = owner_ids * capacity + rank
        slots = jnp.arange(owners * capacity, dtype=jnp.int32)
        selector = (slots[:, None] == place[None, :]).astype(f32)
        by_block = jnp.sum(selector.reshape(-1, block_count, per_block), axis=2)
        outgoing = jnp.einsum("sb,rbx->srx", by_block, atoms, precision=lax.Precision.HIGHEST)
        labels = jnp.sum(selector * (tids.reshape(pair_count)[None] + 1.0), axis=1) - 1.0
        labels = jnp.pad(labels[:, None], ((0, 0), (0, 127)), constant_values=-1.0)
        outgoing = jnp.concatenate([outgoing, labels[:, None]], axis=1)
        arrived = lax.all_to_all(outgoing, OWN, split_axis=0, concat_axis=0, tiled=True)
        wg, res = pair_sums([arrived.transpose(1, 0, 2)], type_table, widths, pts, wts)
        res = lax.psum(res.T, "sub")
        got = lax.all_to_all(res, OWN, split_axis=0, concat_axis=0, tiled=True)
        per_pair = jnp.einsum("sp,sx->px", selector, got[:, :13], precision=lax.Precision.HIGHEST)
        scores = per_pair[:, 0].reshape(block_count, per_block)
        pose_grad = jnp.sum(per_pair[:, 1:].reshape(block_count, per_block, 12), axis=1)
    return scores, pose_grad, wg.reshape(5, tmpl_count, 128).transpose(1, 0, 2)


def solution(mesh):
    in_specs = (
        P(("groups", "lib", "tmpl"), None, None),
        P(("groups", "lib", "tmpl"), None),
        P(("groups", "lib", "tmpl"), None),
        P(("groups", "lib", "tmpl"), None),
        P(("groups", "lib", "tmpl"), None),
        P(("groups", "lib", "tmpl"), None),
        P(),
        P(),
        P(("lib", "tmpl"), None, "sub"),
        P(("lib", "tmpl"), None, "sub"),
    )
    out_specs = (
        P(("groups", "lib", "tmpl"), None),
        P(("groups", "lib", "tmpl"), None),
        P(("groups", "lib", "tmpl"), None, "sub"),
    )
    return jax.shard_map(local, mesh=mesh, in_specs=in_specs, out_specs=out_specs, check_vma=False)
```

```python
import functools
import math
import jax
import jax.numpy as jnp
from jax import lax
from jax.experimental import pallas as pl
from jax.experimental.pallas import tpu as pltpu
from jax.sharding import PartitionSpec as P

bf16, f32, i32 = jnp.bfloat16, jnp.float32, jnp.int32
LOG2E = math.log2(math.e)
OWN = ("lib", "tmpl")
PLANES = 6
PP = 8
VMEM_LIMIT = 36 * 1024 * 1024


def split3(x):
    h = x.astype(bf16).astype(f32)
    r = x - h
    m = r.astype(bf16).astype(f32)
    return h, m, r - m


def split2(x):
    h = x.astype(bf16)
    return h, (x - h.astype(f32)).astype(bf16)


def iota(shape, axis):
    return lax.broadcasted_iota(i32, shape, axis)


def sum_lanes(m):
    h, l = split2(m)
    dims = (((1,), (1,)), ((), ()))
    o = lax.dot_general(jnp.ones((8, 256), bf16), jnp.concatenate([h, l], axis=1), dims, preferred_element_type=f32)
    return o[0:1]


def pair_kernel(*refs, lay):
    blocks, tmpl, rows, groups, srcs_n = lay.blocks, lay.tmpl, lay.rows, lay.groups, lay.arrays
    srcs, refs = refs[:srcs_n], refs[srcs_n:]
    prior, refs = (refs[:2], refs[2:]) if lay.prior else (None, refs)
    const_ref, pts_ref, v_ref, yk_ref, wg_ref, out_ref = refs[:6]
    feats_ref, s_ref, res_ref, idv_ref, ids_ref, sem, idsem = refs[6:13]
    bufs = refs[13:]
    half = len(bufs) // 2
    A, B = bufs[:half], bufs[half:]
    each = groups // srcs_n
    copies = [pltpu.make_async_copy(x, feats_ref.at[pl.ds(k * each, each)], sem.at[k]) for k, x in enumerate(srcs)]
    for c in copies:
        c.start()
    wg_ref[...] = prior[0][...] if lay.prior else jnp.zeros_like(wg_ref)
    for r in A + B:
        r[...] = jnp.zeros_like(r)
    width = [jnp.broadcast_to(const_ref[f : f + 1, :], (8, 128)) for f in range(5)]
    force = [-2.0 * w for w in width]
    s0 = -LOG2E * width[0]
    ratio = (width[1] / width[0])[0:1]
    row8 = iota((8, 128), 0)
    lane8 = iota((8, 128), 1)
    by_chan = jnp.where(lane8 < 16, force[2], jnp.where(lane8 < 32, force[3], force[4]))
    top = row8 == 0
    tab0 = jnp.broadcast_to(const_ref[5:6, :], (8, 128)) * jnp.where(top, 1.0, force[0])
    tab1 = jnp.broadcast_to(const_ref[6:7, :], (8, 128)) * jnp.where(top, 1.0, by_chan)
    tabs = -LOG2E * jnp.where(lane8 == 0, width[2], jnp.where(lane8 == 1, width[3], width[4]))
    charge_scale = jnp.where(top, 1.0, force[1])
    chan_of_row = jnp.where((row8 > 0) & (row8 < 7), (row8 - 1) // 2, -1).astype(f32)

    for c in copies:
        c.wait()
    owner = lax.axis_index("lib") * lax.axis_size("tmpl") + lax.axis_index("tmpl")
    near = feats_ref[:, PLANES * rows : PLANES * rows + 8, :] - (owner * tmpl).astype(f32)
    named = (near >= 0.0) & (near < float(tmpl)) & (iota(near.shape, 1) < 4)
    idv_ref[...] = jnp.max(jnp.where(named, near + 1.0, 0.0), axis=1).astype(i32) - 1
    copy = pltpu.make_async_copy(idv_ref, ids_ref, idsem)
    copy.start()
    copy.wait()

    def slot(b0, u):
        g = lax.div(b0, rows)
        base = 0 if lay.dense else rows * lax.rem(lax.div(g, each) + lax.axis_index("sub"), 2)
        t = ids_ref[g, base + lax.rem(b0, rows) + u]
        return jnp.maximum(t, 0), t >= 0

    def stage0(b0, xt_ref, w_ref):
        for u in range(PP // 2):
            cols = []
            for k in range(2):
                _, valid = slot(b0, 2 * u + k)
                off = jnp.where(valid, 0.0, 64.0)

                def row(q):
                    at_ = q * rows + lax.rem(b0, rows) + 2 * u + k
                    return jnp.broadcast_to(feats_ref[lax.div(b0, rows), pl.ds(at_, 1), :], (8, 128))

                x0, x1, x2 = row(0), row(1), row(2)
                chan = row(5)
                kind = row(4) + off
                steric = jnp.take_along_axis(tab0, kind.astype(i32), axis=1)
                strength = jnp.take_along_axis(tab1, (kind + 16.0 * chan).astype(i32), axis=1)
                sph = jnp.take_along_axis(tabs, chan.astype(i32), axis=1)
                charge = row(3) * (charge_scale * valid.astype(f32))
                p = jnp.where((row8 == 1) | (row8 == 4) | (row8 == 7), x0, jnp.where((row8 == 2) | (row8 == 5), x1,
                    jnp.where((row8 == 3) | (row8 == 6), x2, 1.0)))
                q = jnp.where(row8 == 4, x0, jnp.where((row8 == 5) | (row8 == 7), x1, jnp.where(row8 == 6, x2, 1.0)))
                lo8 = p * q
                cross = jnp.where(lax.rem(row8, 2) == 1, x0, x1) * x2
                hi8 = jnp.where((row8 == 1) | (row8 == 2), cross, jnp.where(row8 == 7, 1.0, 0.0))
                parts_ = []
                for sc in (s0, sph):
                    h, m, l = split3(lo8 * sc)
                    parts_.append(jnp.concatenate([h, h, h, m, m, l], axis=0))
                cols.append(jnp.concatenate(parts_, axis=1))
                z = lo8 * strength
                zs = [jnp.where(chan == float(c), z, 0.0) for c in range(3)]
                zs.append(jnp.where(chan == chan_of_row, strength * cross, 0.0))
                ws = [[lo8 * steric, hi8 * steric], [lo8 * charge, hi8 * charge], zs]
                ws = [split2(jnp.concatenate(w, axis=0)) for w in ws]
                w_ref[2 * u + k] = jnp.concatenate([x for pair in ws for x in pair], axis=0)
            xt_ref[u] = jnp.concatenate(cols, axis=0).astype(bf16).T

    def stage1(b0, xt_ref, a_ref):
        for u in range(PP // 2):
            rhs = []
            for k in range(2):
                t, _ = slot(b0, 2 * u + k)
                yk = yk_ref[pl.ds(pl.multiple_of(t * 48, 16), 48), :]
                z = jnp.zeros_like(yk)
                rhs.append(jnp.concatenate([yk, z] if k == 0 else [z, yk], axis=1))
            a_ref[u] = jnp.dot(xt_ref[u], jnp.concatenate(rhs, axis=0), preferred_element_type=f32)

    def stage2(a_ref, w_ref, r_ref):
        for q in range(PP):
            js = slice(128 * (q % 2), 128 * (q % 2) + 128)

            def contract(e, at, n):
                eh, el = split2(e)
                w = w_ref[q, at : at + 2 * n]
                o = jnp.dot(jnp.concatenate([w, w], axis=1), jnp.concatenate([eh, el], axis=0), preferred_element_type=f32)
                return o[:n] + o[n:]

            a0 = a_ref[q // 2, 0:128, js]
            r_ref[q, 0:16] = contract(jnp.exp2(a0), 0, 16)
            r_ref[q, 16:32] = contract(jnp.exp2(a0 * ratio), 32, 16)
            r_ref[q, 32:64] = contract(jnp.exp2(a_ref[q // 2, 128:256, js]), 64, 32)

    def stage3(b0, r_ref):
        for q in range(PP):
            t, _ = slot(b0, q)
            b = b0 + q
            v = [jnp.broadcast_to(v_ref[pl.ds(f * tmpl + t, 1), :], (8, 128)) for f in range(5)]
            r = [r_ref[q, 8 * k : 8 * k + 8] for k in range(8)]
            z = [r[4 + c] * v[2 + c] for c in range(3)]
            lo = r[0] * v[0] + r[2] * v[1] + (z[0] + z[1] + z[2])
            t0 = z[0] * force[2] + z[1] * force[3] + z[2] * force[4]
            hi = r[1] * v[0] + r[3] * v[1] + r[7] * jnp.where(row8 < 3, v[2], jnp.where(row8 < 5, v[3], v[4]))
            for f, k in enumerate((0, 2, 4, 5, 6)):
                dst = pl.ds(f * tmpl + t, 1)
                wg_ref[dst, :] = wg_ref[dst, :] + r[k][0:1]
            rows_ = [lo[n : n + 1] for n in range(8)] + [t0[0:1]] + [hi[n : n + 1] for n in range(1, 8)]
            rows_ += [pts_ref[pl.ds(c * tmpl + t, 1), :] for c in range(3)]
            for n, x in enumerate(rows_):
                s_ref[pl.ds(n * blocks + b, 1), :] = x

    n = blocks // PP

    def at(i):
        return jnp.clip(i, 0, n - 1) * PP

    def halfstep(i, src, dst):
        xt_s, a_s, w_s, r_s = src
        xt_d, a_d, w_d, r_d = dst
        stage3(at(i - 3), r_s)
        stage2(a_s, w_d, r_d)
        stage1(at(i - 1), xt_s, a_d)
        stage0(at(i), xt_d, w_d)

    def step(i, _):
        halfstep(2 * i, A, B)
        halfstep(2 * i + 1, B, A)
        return 0

    lax.fori_loop(0, (n + 2) // 2, step, 0)
    stage3((n - 1) * PP, A[-1])

    def col(k):
        return s_ref[k * blocks : (k + 1) * blocks, :]

    y = [col(16 + c) for c in range(3)]
    xz, yz = col(9) + col(11) + col(13), col(10) + col(12) + col(14)
    second = [[col(4), col(7), xz], [col(7), col(5), yz], [xz, yz, col(6)]]
    t0 = col(8) + col(15)
    res_ref[...] = jnp.zeros_like(res_ref)
    res_ref[0:1, 0:blocks] = sum_lanes(col(0))
    for c in range(3):
        res_ref[1 + c : 2 + c, 0:blocks] = sum_lanes(col(1 + c) - y[c] * t0)
        for d in range(3):
            k = 4 + 3 * c + d
            res_ref[k : k + 1, 0:blocks] = sum_lanes(second[c][d] - y[c] * col(1 + d))
    if lay.dense:
        out_ref[...] = res_ref[:, 0:blocks]
        return
    out_ref[...] = prior[1][...] if lay.prior else jnp.zeros_like(out_ref)
    lib, tm = lax.axis_index("lib"), lax.axis_index("tmpl")
    libs, tms = lax.axis_size("lib"), lax.axis_size("tmpl")
    for a in range(srcs_n // 2):
        for q in range(each):
            piece = None
            for k in range(2):
                for h in range(2):
                    start, to = ((2 * a + h) * each + q) * rows, (2 * k + h) * rows
                    x = res_ref[8 * k : 8 * k + 8, start // 128 * 128 : start // 128 * 128 + 128]
                    shift = (to - start) % 128
                    x = pltpu.roll(x, shift, 1) if shift else x
                    piece = x if piece is None else jnp.where(lane8 < to, piece, x)
            chip = lax.rem(lib + libs - lay.shifts[a], libs) * tms + lax.rem(tm + tms - q, tms)
            for s in range(2):
                out_ref[2 * chip + s] = piece


class Layout:
    def __init__(self, feats, tmpl, shifts, prior):
        self.arrays, self.tmpl, self.shifts, self.prior = len(feats), tmpl, shifts, prior
        self.dense = not shifts
        self.groups = sum(x.shape[0] for x in feats)
        self.rows = (feats[0].shape[1] - 8) // PLANES
        self.blocks = self.groups * self.rows


def pair_sums(feats, consts, templates, shifts=(), out=None, prior=None):
    lay = Layout(feats, templates[0].shape[0] // 3, shifts, prior is not None)
    blocks, tmpl, groups = lay.blocks, lay.tmpl, lay.groups
    out = out or (16, blocks)
    hbm, vmem = (pl.BlockSpec(memory_space=m) for m in (pl.ANY, pltpu.VMEM))
    stages = [
        pltpu.VMEM((PP // 2, 256, 96), bf16),
        pltpu.VMEM((PP // 2, 256, 256), f32),
        pltpu.VMEM((PP, 128, 128), bf16),
        pltpu.VMEM((PP, 64, 128), f32),
    ]
    elements = blocks * 128 * 128
    return pl.pallas_call(
        functools.partial(pair_kernel, lay=lay),
        out_shape=(jax.ShapeDtypeStruct((5 * tmpl, 128), f32), jax.ShapeDtypeStruct(out, f32)),
        in_specs=[hbm] * len(feats) + [vmem] * (2 * lay.prior) + [vmem] * 4,
        out_specs=(vmem, vmem),
        scratch_shapes=[
            pltpu.VMEM((groups,) + feats[0].shape[1:], f32),
            pltpu.VMEM((19 * blocks, 128), f32),
            pltpu.VMEM((16, -(-blocks // 128) * 128), f32),
            pltpu.VMEM((groups, 128), i32),
            pltpu.SMEM((groups, 128), i32),
            pltpu.SemaphoreType.DMA((len(feats),)),
            pltpu.SemaphoreType.DMA,
        ] + stages + stages,
        compiler_params=pltpu.CompilerParams(vmem_limit_bytes=VMEM_LIMIT),
        cost_estimate=pl.CostEstimate(flops=700 * elements, bytes_accessed=10 * elements // 8, transcendentals=3 * elements),
        name="gauss",
    )(*feats, *(prior or ()), consts, *templates)


def template_kernel(pts_ref, wts_ref, pts_out, v_ref, yk_ref):
    tmpl = pts_ref.shape[0] // 3
    pts_out[...] = pts_ref[...]
    v_ref[...] = wts_ref[...].astype(f32)
    row8 = iota((8, 128), 0)

    def step(i, _):
        for u in range(8):
            t = i * 8 + u
            y = [jnp.broadcast_to(pts_ref[pl.ds(c * tmpl + t, 1), :], (8, 128)) for c in range(3)]
            sq = y[0] * y[0] + y[1] * y[1] + y[2] * y[2]
            yf = jnp.where(row8 == 0, sq, jnp.where(row8 < 4, -2.0 * jnp.where(row8 == 1, y[0], jnp.where(row8 == 2, y[1], y[2])),
                 jnp.where(row8 < 7, 1.0, 0.0)))
            h, m, l = split3(yf)
            yk_ref[pl.ds(pl.multiple_of(t * 48, 16), 48), :] = jnp.concatenate([h, m, l, h, m, h], axis=0).astype(bf16)
        return 0

    lax.fori_loop(0, tmpl // 8, step, 0)


def const_rows(widths_ref, table_ref, const_ref):
    const_ref[...] = jnp.zeros_like(const_ref)
    kinds = table_ref.shape[1]
    for f in range(5):
        const_ref[f : f + 1, :] = jnp.broadcast_to(widths_ref[0:1, f : f + 1], (1, 128))
    const_ref[5:6, 0:kinds] = table_ref[0:1, :]
    for c in range(3):
        const_ref[6:7, kinds * c : kinds * (c + 1)] = table_ref[1:2, :]


def pack_kernel(xyz_ref, charge_ref, kind_ref, chan_ref, owner_ref, slot_ref, widths_ref, table_ref, out_ref, const_ref, *, tmpl):
    const_rows(widths_ref, table_ref, const_ref)
    rows = (out_ref.shape[0] - 8) // PLANES
    mine = pl.ds(pl.multiple_of(lax.axis_index("sub") * rows, rows), rows)
    planes = [xyz_ref[c, mine, :] for c in range(3)]
    planes += [charge_ref[mine, :], kind_ref[mine, :].astype(f32), chan_ref[mine, :].astype(f32)]
    top, count = owner_ref.shape
    for k, x in enumerate(planes):
        out_ref[k * rows : (k + 1) * rows, :] = x
    out_ref[PLANES * rows :, :] = jnp.full((8, 128), -1.0, f32)
    out_ref[PLANES * rows : PLANES * rows + top, 0:count] = (owner_ref[...] * tmpl + slot_ref[...]).astype(f32)


def merge_kernel(got_ref, owner_ref, scores_ref, pose_ref):
    top, count = owner_ref.shape
    rows = count // 2
    lane = iota((8, 128), 1)
    total = None
    owner = owner_ref[...]
    scores = jnp.zeros((top, count), f32)
    for o in range(got_ref.shape[0] // 2):
        other = got_ref[2 * o + 1]
        other = jnp.where(lax.rem(lane, count) < rows, pltpu.roll(other, 128 - rows, 1), pltpu.roll(other, rows, 1))
        both = got_ref[2 * o] + other
        total = both if total is None else total + both
        scores = scores + jnp.where(owner == o, both[0:1, 0:count], 0.0)
    scores_ref[...] = scores
    pose_ref[0:7, :] = total[1:8, 0:count]
    pose_ref[7:12, :] = pltpu.roll(total, 128 - count, 1)[0:5, 0:count]


def local(coords, atom_type, channel, charge, pair_owner, pair_slot, type_table, widths, tmpl_points, tmpl_weights):
    block_count, per_block = pair_owner.shape
    tmpl_count = tmpl_points.shape[0]
    owners = lax.axis_size(OWN)
    pair_count = block_count * per_block
    capacity = max(2, 2 * pair_count // owners)
    pts = tmpl_points.transpose(1, 0, 2).reshape(3 * tmpl_count, 128)
    wts = tmpl_weights.transpose(1, 0, 2).reshape(5 * tmpl_count, 128)
    templates = pl.pallas_call(
        template_kernel,
        out_shape=(
            jax.ShapeDtypeStruct(pts.shape, f32),
            jax.ShapeDtypeStruct(wts.shape, f32),
            jax.ShapeDtypeStruct((48 * tmpl_count, 128), bf16),
        ),
        compiler_params=pltpu.CompilerParams(vmem_limit_bytes=VMEM_LIMIT),
        cost_estimate=pl.CostEstimate(flops=4000 * 128 * tmpl_count, bytes_accessed=8000 * tmpl_count, transcendentals=0),
        name="templates",
    )(pts, wts)
    if capacity >= block_count:
        rows = block_count // 2
        mine, consts = pl.pallas_call(
            functools.partial(pack_kernel, tmpl=tmpl_count),
            out_shape=(jax.ShapeDtypeStruct((PLANES * rows + 8, 128), f32), jax.ShapeDtypeStruct((8, 128), f32)),
            name="pack",
        )(coords.transpose(1, 0, 2), charge, atom_type, channel, pair_owner.T, pair_slot.T, widths[None], type_table.T)

        def shifted(x, axis, k):
            size = lax.axis_size(axis)
            return lax.ppermute(x, axis, [(i, (i + k) % size) for i in range(size)])

        partners = [shifted(mine, "tmpl", k) for k in range(1, lax.axis_size("tmpl"))]
        partners, templates = lax.optimization_barrier((partners, templates))
        near = jnp.stack([mine] + partners)
        lib_shifts = tuple(range(1, lax.axis_size("lib")))
        far = [shifted(near, "lib", k) for k in lib_shifts]
        near = [near, shifted(near, "sub", 1)]
        shape = (2 * owners, 8, 128)
        done = pair_sums(near, consts, templates, (0,), shape)
        far, done = lax.optimization_barrier((far, done))
        far = [x for y in far for x in (y, shifted(y, "sub", 1))]
        wg, out = pair_sums(far, consts, templates, lib_shifts, shape, done)
        got = lax.all_to_all(out, OWN + ("sub",), split_axis=0, concat_axis=0, tiled=True)
        scores, pose_grad = pl.pallas_call(
            merge_kernel,
            out_shape=(jax.ShapeDtypeStruct((per_block, block_count), f32), jax.ShapeDtypeStruct((12, block_count), f32)),
            name="merge",
        )(got, pair_owner.T)
        scores, pose_grad = scores.T, pose_grad.T
    else:
        consts = pl.pallas_call(const_rows, out_shape=jax.ShapeDtypeStruct((8, 128), f32), name="consts")(widths[None], type_table.T)
        tids = (pair_owner * tmpl_count + pair_slot).astype(f32)
        atoms = jnp.concatenate(
            [coords.transpose(1, 0, 2), jnp.stack([charge, atom_type.astype(f32), channel.astype(f32)])], axis=0
        )
        owner_ids = pair_owner.reshape(pair_count)
        order = jnp.arange(pair_count, dtype=i32)
        earlier = (owner_ids[None, :] == owner_ids[:, None]) & (order[None, :] < order[:, None])
        rank = jnp.sum(earlier.astype(i32), axis=1)
        place = owner_ids * capacity + rank
        slots = jnp.arange(owners * capacity, dtype=i32)
        selector = (slots[:, None] == place[None, :]).astype(f32)
        by_block = jnp.sum(selector.reshape(-1, block_count, per_block), axis=2)
        outgoing = jnp.einsum("sb,rbx->srx", by_block, atoms, precision=lax.Precision.HIGHEST)
        labels = jnp.sum(selector * (tids.reshape(pair_count)[None] + 1.0), axis=1) - 1.0
        labels = jnp.pad(labels[:, None], ((0, 0), (0, 127)), constant_values=-1.0)
        outgoing = jnp.concatenate([outgoing, labels[:, None]], axis=1)
        arrived = lax.all_to_all(outgoing, OWN, split_axis=0, concat_axis=0, tiled=True)
        groups = 16
        rows = owners * capacity // groups
        atoms = arrived[:, :PLANES].reshape(groups, rows, PLANES, 128).transpose(0, 2, 1, 3).reshape(groups, PLANES * rows, 128)
        ids = arrived[:, PLANES, 0].reshape(groups, 1, rows)
        ids = jnp.pad(ids, ((0, 0), (0, 7), (0, 128 - rows)), constant_values=-1.0)
        wg, res = pair_sums([jnp.concatenate([atoms, ids], axis=1)], consts, templates)
        res = lax.psum(res.T, "sub")
        got = lax.all_to_all(res, OWN, split_axis=0, concat_axis=0, tiled=True)
        per_pair = jnp.einsum("sp,sx->px", selector, got[:, :13], precision=lax.Precision.HIGHEST)
        scores = per_pair[:, 0].reshape(block_count, per_block)
        pose_grad = jnp.sum(per_pair[:, 1:].reshape(block_count, per_block, 12), axis=1)
    return scores, pose_grad, wg.reshape(5, tmpl_count, 128).transpose(1, 0, 2)


def solution(mesh):
    in_specs = (
        P(("groups", "lib", "tmpl"), None, None),
        P(("groups", "lib", "tmpl"), None),
        P(("groups", "lib", "tmpl"), None),
        P(("groups", "lib", "tmpl"), None),
        P(("groups", "lib", "tmpl"), None),
        P(("groups", "lib", "tmpl"), None),
        P(),
        P(),
        P(("lib", "tmpl"), None, "sub"),
        P(("lib", "tmpl"), None, "sub"),
    )
    out_specs = (
        P(("groups", "lib", "tmpl"), None),
        P(("groups", "lib", "tmpl"), None),
        P(("groups", "lib", "tmpl"), None, "sub"),
    )
    return jax.shard_map(local, mesh=mesh, in_specs=in_specs, out_specs=out_specs, check_vma=False)
```

```python
import functools
import math
import jax
import jax.numpy as jnp
from jax import lax
from jax.experimental import pallas as pl
from jax.experimental.pallas import tpu as pltpu
from jax.sharding import PartitionSpec as P

bf16, f32, i32 = jnp.bfloat16, jnp.float32, jnp.int32
LOG2E = math.log2(math.e)
OWN = ("lib", "tmpl")
PLANES = 6
PP = 8
UNROLL = 4
VMEM_LIMIT = 36 * 1024 * 1024
TEMPLATE_LIMIT = 36 * 1024 * 1024


def split3(x):
    h = x.astype(bf16).astype(f32)
    r = x - h
    m = r.astype(bf16).astype(f32)
    return h, m, r - m


def split2(x):
    h = x.astype(bf16)
    return h, (x - h.astype(f32)).astype(bf16)


def iota(shape, axis):
    return lax.broadcasted_iota(i32, shape, axis)


def sum_lanes(m):
    h, l = split2(m)
    dims = (((1,), (1,)), ((), ()))
    o = lax.dot_general(jnp.ones((8, 256), bf16), jnp.concatenate([h, l], axis=1), dims, preferred_element_type=f32)
    return o[0:1]


def pair_kernel(*refs, lay):
    blocks, tmpl, rows, groups, srcs_n = lay.blocks, lay.tmpl, lay.rows, lay.groups, lay.arrays
    srcs, refs = refs[:srcs_n], refs[srcs_n:]
    prior, refs = (refs[:2], refs[2:]) if lay.prior else (None, refs)
    const_ref, pts_ref, v_ref, yk_ref, wg_ref, out_ref = refs[:6]
    feats_ref, s_ref, res_ref, idv_ref, ids_ref, sem, idsem = refs[6:13]
    bufs = refs[13:]
    half = len(bufs) // 2
    A, B = bufs[:half], bufs[half:]
    each = groups // srcs_n
    copies = [pltpu.make_async_copy(x, feats_ref.at[pl.ds(k * each, each)], sem.at[k]) for k, x in enumerate(srcs)]
    for c in copies:
        c.start()
    wg_ref[...] = prior[0][...] if lay.prior else jnp.zeros_like(wg_ref)
    width = [jnp.broadcast_to(const_ref[f : f + 1, :], (8, 128)) for f in range(5)]
    force = [-2.0 * w for w in width]
    s0 = -LOG2E * width[0]
    ratio = (width[1] / width[0])[0:1]
    row8 = iota((8, 128), 0)
    lane8 = iota((8, 128), 1)
    by_chan = jnp.where(lane8 < 16, force[2], jnp.where(lane8 < 32, force[3], force[4]))
    top = row8 == 0
    tab0 = jnp.broadcast_to(const_ref[5:6, :], (8, 128)) * jnp.where(top, 1.0, force[0])
    tab1 = jnp.broadcast_to(const_ref[6:7, :], (8, 128)) * jnp.where(top, 1.0, by_chan)
    tabs = -LOG2E * jnp.where(lane8 == 0, width[2], jnp.where(lane8 == 1, width[3], width[4]))
    charge_scale = jnp.where(top, 1.0, force[1])
    chan_of_row = jnp.where((row8 > 0) & (row8 < 7), (row8 - 1) // 2, -1).astype(f32)

    for c in copies:
        c.wait()
    owner = lax.axis_index("lib") * lax.axis_size("tmpl") + lax.axis_index("tmpl")
    near = feats_ref[:, PLANES * rows : PLANES * rows + 8, :] - (owner * tmpl).astype(f32)
    named = (near >= 0.0) & (near < float(tmpl)) & (iota(near.shape, 1) < 4)
    idv_ref[...] = jnp.max(jnp.where(named, near + 1.0, 0.0), axis=1).astype(i32) - 1
    copy = pltpu.make_async_copy(idv_ref, ids_ref, idsem)
    copy.start()
    copy.wait()

    def slot(b0, u):
        g = lax.div(b0, rows)
        base = 0 if lay.dense else rows * lax.rem(lax.div(g, each) + lax.axis_index("sub"), 2)
        t = ids_ref[g, base + lax.rem(b0, rows) + u]
        return jnp.maximum(t, 0), t >= 0

    def stage0(b0, xt_ref, w_ref):
        for u in range(PP // 2):
            cols = []
            for k in range(2):
                _, valid = slot(b0, 2 * u + k)
                off = jnp.where(valid, 0.0, 64.0)

                def row(q):
                    at_ = q * rows + lax.rem(b0, rows) + 2 * u + k
                    return jnp.broadcast_to(feats_ref[lax.div(b0, rows), pl.ds(at_, 1), :], (8, 128))

                x0, x1, x2 = row(0), row(1), row(2)
                chan = row(5)
                kind = row(4) + off
                steric = jnp.take_along_axis(tab0, kind.astype(i32), axis=1)
                strength = jnp.take_along_axis(tab1, (kind + 16.0 * chan).astype(i32), axis=1)
                sph = jnp.take_along_axis(tabs, chan.astype(i32), axis=1)
                charge = row(3) * (charge_scale * valid.astype(f32))
                p = jnp.where((row8 == 1) | (row8 == 4) | (row8 == 7), x0, jnp.where((row8 == 2) | (row8 == 5), x1,
                    jnp.where((row8 == 3) | (row8 == 6), x2, 1.0)))
                q = jnp.where(row8 == 4, x0, jnp.where((row8 == 5) | (row8 == 7), x1, jnp.where(row8 == 6, x2, 1.0)))
                lo8 = p * q
                cross = jnp.where(lax.rem(row8, 2) == 1, x0, x1) * x2
                hi8 = jnp.where((row8 == 1) | (row8 == 2), cross, jnp.where(row8 == 7, 1.0, 0.0))
                parts_ = []
                for sc in (s0, sph):
                    h, m, l = split3(lo8 * sc)
                    parts_.append(jnp.concatenate([h, h, h, m, m, l], axis=0))
                cols.append(jnp.concatenate(parts_, axis=1))
                z = lo8 * strength
                zs = [jnp.where(chan == float(c), z, 0.0) for c in range(3)]
                zs.append(jnp.where(chan == chan_of_row, strength * cross, 0.0))
                ws = [[lo8 * steric, hi8 * steric], [lo8 * charge, hi8 * charge], zs]
                ws = [split2(jnp.concatenate(w, axis=0)) for w in ws]
                w_ref[2 * u + k] = jnp.concatenate([x for pair in ws for x in pair], axis=0)
            xt_ref[u] = jnp.concatenate(cols, axis=0).astype(bf16).T

    def stage1(b0, xt_ref, a_ref):
        for u in range(PP // 2):
            rhs = []
            for k in range(2):
                t, _ = slot(b0, 2 * u + k)
                yk = yk_ref[pl.ds(pl.multiple_of(t * 48, 16), 48), :]
                z = jnp.zeros_like(yk)
                rhs.append(jnp.concatenate([yk, z] if k == 0 else [z, yk], axis=1))
            a_ref[u] = jnp.dot(xt_ref[u], jnp.concatenate(rhs, axis=0), preferred_element_type=f32)

    def stage2(a_ref, w_ref, r_ref):
        for q in range(PP):
            js = slice(128 * (q % 2), 128 * (q % 2) + 128)

            def contract(e, at, n):
                eh, el = split2(e)
                w = w_ref[q, at : at + 2 * n]
                o = jnp.dot(jnp.concatenate([w, w], axis=1), jnp.concatenate([eh, el], axis=0), preferred_element_type=f32)
                return o[:n] + o[n:]

            a0 = a_ref[q // 2, 0:128, js]
            r_ref[q, 0:16] = contract(jnp.exp2(a0), 0, 16)
            r_ref[q, 16:32] = contract(jnp.exp2(a0 * ratio), 32, 16)
            r_ref[q, 32:64] = contract(jnp.exp2(a_ref[q // 2, 128:256, js]), 64, 32)

    def stage3(b0, r_ref):
        for q in range(PP):
            t, _ = slot(b0, q)
            b = b0 + q
            v = [jnp.broadcast_to(v_ref[pl.ds(f * tmpl + t, 1), :], (8, 128)) for f in range(5)]
            r = [r_ref[q, 8 * k : 8 * k + 8] for k in range(8)]
            z = [r[4 + c] * v[2 + c] for c in range(3)]
            lo = r[0] * v[0] + r[2] * v[1] + (z[0] + z[1] + z[2])
            t0 = z[0] * force[2] + z[1] * force[3] + z[2] * force[4]
            hi = r[1] * v[0] + r[3] * v[1] + r[7] * jnp.where(row8 < 3, v[2], jnp.where(row8 < 5, v[3], v[4]))
            for f, k in enumerate((0, 2, 4, 5, 6)):
                dst = pl.ds(f * tmpl + t, 1)
                wg_ref[dst, :] = wg_ref[dst, :] + r[k][0:1]
            rows_ = [lo[n : n + 1] for n in range(8)] + [t0[0:1]] + [hi[n : n + 1] for n in range(1, 8)]
            rows_ += [pts_ref[pl.ds(c * tmpl + t, 1), :] for c in range(3)]
            for n, x in enumerate(rows_):
                s_ref[pl.ds(n * blocks + b, 1), :] = x

    n = blocks // PP

    def halfstep(i, stages=(3, 2, 1, 0), even=None):
        src, dst = (A, B) if even else (B, A)
        xt_s, a_s, w_s, r_s = src
        xt_d, a_d, w_d, r_d = dst
        if 3 in stages:
            stage3((i - 3) * PP, r_s)
        if 2 in stages:
            stage2(a_s, w_d, r_d)
        if 1 in stages:
            stage1((i - 1) * PP, xt_s, a_d)
        if 0 in stages:
            stage0(i * PP, xt_d, w_d)

    def step(k, _):
        for u in range(UNROLL):
            halfstep(first + UNROLL * k + u, even=(first + u) % 2 == 0)
        return 0

    first = min(n, 3)
    while (n - first) % UNROLL or UNROLL % 2:
        first += 1
    for i in range(first):
        halfstep(i, [q for q in range(3, -1, -1) if i >= q], i % 2 == 0)
    if n > first:
        lax.fori_loop(0, (n - first) // UNROLL, step, 0)
    for i in range(n, n + 3):
        halfstep(i, [q for q in range(3, 0, -1) if i - q < n], i % 2 == 0)

    def col(k):
        return s_ref[k * blocks : (k + 1) * blocks, :]

    y = [col(16 + c) for c in range(3)]
    xz, yz = col(9) + col(11) + col(13), col(10) + col(12) + col(14)
    second = [[col(4), col(7), xz], [col(7), col(5), yz], [xz, yz, col(6)]]
    t0 = col(8) + col(15)
    res_ref[...] = jnp.zeros_like(res_ref)
    res_ref[0:1, 0:blocks] = sum_lanes(col(0))
    for c in range(3):
        res_ref[1 + c : 2 + c, 0:blocks] = sum_lanes(col(1 + c) - y[c] * t0)
        for d in range(3):
            k = 4 + 3 * c + d
            res_ref[k : k + 1, 0:blocks] = sum_lanes(second[c][d] - y[c] * col(1 + d))
    if lay.dense:
        out_ref[...] = res_ref[:, 0:blocks]
        return
    out_ref[...] = prior[1][...] if lay.prior else jnp.zeros_like(out_ref)
    lib, tm = lax.axis_index("lib"), lax.axis_index("tmpl")
    libs, tms = lax.axis_size("lib"), lax.axis_size("tmpl")
    for q, (up, over) in enumerate(lay.chips):
        piece = None
        for k in range(2):
            for h in range(2):
                start, to = (h * each + q) * rows, (2 * k + h) * rows
                x = res_ref[8 * k : 8 * k + 8, start // 128 * 128 : start // 128 * 128 + 128]
                shift = (to - start) % 128
                x = pltpu.roll(x, shift, 1) if shift else x
                piece = x if piece is None else jnp.where(lane8 < to, piece, x)
        chip = lax.rem(lib + libs - up, libs) * tms + lax.rem(tm + tms - over, tms)
        for s in range(2):
            out_ref[2 * chip + s] = piece


class Layout:
    def __init__(self, feats, tmpl, chips, prior):
        self.arrays, self.tmpl, self.chips, self.prior = len(feats), tmpl, chips, prior
        self.dense = not chips
        self.groups = sum(x.shape[0] for x in feats)
        self.rows = (feats[0].shape[1] - 8) // PLANES
        self.blocks = self.groups * self.rows


def pair_sums(feats, consts, templates, chips=(), out=None, prior=None):
    lay = Layout(feats, templates[0].shape[0] // 3, chips, prior is not None)
    blocks, tmpl, groups = lay.blocks, lay.tmpl, lay.groups
    out = out or (16, blocks)
    hbm, vmem = (pl.BlockSpec(memory_space=m) for m in (pl.ANY, pltpu.VMEM))
    stages = [
        pltpu.VMEM((PP // 2, 256, 96), bf16),
        pltpu.VMEM((PP // 2, 256, 256), f32),
        pltpu.VMEM((PP, 128, 128), bf16),
        pltpu.VMEM((PP, 64, 128), f32),
    ]
    elements = blocks * 128 * 128
    return pl.pallas_call(
        functools.partial(pair_kernel, lay=lay),
        out_shape=(jax.ShapeDtypeStruct((5 * tmpl, 128), f32), jax.ShapeDtypeStruct(out, f32)),
        in_specs=[hbm] * len(feats) + [vmem] * (2 * lay.prior) + [vmem] * 4,
        out_specs=(vmem, vmem),
        scratch_shapes=[
            pltpu.VMEM((groups,) + feats[0].shape[1:], f32),
            pltpu.VMEM((19 * blocks, 128), f32),
            pltpu.VMEM((16, -(-blocks // 128) * 128), f32),
            pltpu.VMEM((groups, 128), i32),
            pltpu.SMEM((groups, 128), i32),
            pltpu.SemaphoreType.DMA((len(feats),)),
            pltpu.SemaphoreType.DMA,
        ] + stages + stages,
        compiler_params=pltpu.CompilerParams(vmem_limit_bytes=VMEM_LIMIT),
        cost_estimate=pl.CostEstimate(flops=700 * elements, bytes_accessed=10 * elements // 8, transcendentals=3 * elements),
        name="gauss",
    )(*feats, *(prior or ()), consts, *templates)


def template_kernel(pts_ref, wts_ref, pts_out, v_ref, yk_ref):
    tmpl = pts_ref.shape[0] // 3
    pts_out[...] = pts_ref[...]
    v_ref[...] = wts_ref[...].astype(f32)
    row8 = iota((8, 128), 0)

    def step(i, _):
        for u in range(8):
            t = i * 8 + u
            y = [jnp.broadcast_to(pts_ref[pl.ds(c * tmpl + t, 1), :], (8, 128)) for c in range(3)]
            sq = y[0] * y[0] + y[1] * y[1] + y[2] * y[2]
            yf = jnp.where(row8 == 0, sq, jnp.where(row8 < 4, -2.0 * jnp.where(row8 == 1, y[0], jnp.where(row8 == 2, y[1], y[2])),
                 jnp.where(row8 < 7, 1.0, 0.0)))
            h, m, l = split3(yf)
            yk_ref[pl.ds(pl.multiple_of(t * 48, 16), 48), :] = jnp.concatenate([h, m, l, h, m, h], axis=0).astype(bf16)
        return 0

    lax.fori_loop(0, tmpl // 8, step, 0)


def const_rows(widths_ref, table_ref, const_ref):
    const_ref[...] = jnp.zeros_like(const_ref)
    kinds = table_ref.shape[1]
    for f in range(5):
        const_ref[f : f + 1, :] = jnp.broadcast_to(widths_ref[0:1, f : f + 1], (1, 128))
    const_ref[5:6, 0:kinds] = table_ref[0:1, :]
    for c in range(3):
        const_ref[6:7, kinds * c : kinds * (c + 1)] = table_ref[1:2, :]


def pack_kernel(xyz_ref, charge_ref, kind_ref, chan_ref, owner_ref, slot_ref, widths_ref, table_ref, out_ref, const_ref, *, tmpl):
    const_rows(widths_ref, table_ref, const_ref)
    rows = (out_ref.shape[0] - 8) // PLANES
    mine = pl.ds(pl.multiple_of(lax.axis_index("sub") * rows, rows), rows)
    planes = [xyz_ref[c, mine, :] for c in range(3)]
    planes += [charge_ref[mine, :], kind_ref[mine, :].astype(f32), chan_ref[mine, :].astype(f32)]
    top, count = owner_ref.shape
    for k, x in enumerate(planes):
        out_ref[k * rows : (k + 1) * rows, :] = x
    out_ref[PLANES * rows :, :] = jnp.full((8, 128), -1.0, f32)
    out_ref[PLANES * rows : PLANES * rows + top, 0:count] = (owner_ref[...] * tmpl + slot_ref[...]).astype(f32)


def merge_kernel(got_ref, owner_ref, scores_ref, pose_ref):
    top, count = owner_ref.shape
    rows = count // 2
    lane = iota((8, 128), 1)
    total = None
    owner = owner_ref[...]
    scores = jnp.zeros((top, count), f32)
    for o in range(got_ref.shape[0] // 2):
        other = got_ref[2 * o + 1]
        other = jnp.where(lax.rem(lane, count) < rows, pltpu.roll(other, 128 - rows, 1), pltpu.roll(other, rows, 1))
        both = got_ref[2 * o] + other
        total = both if total is None else total + both
        scores = scores + jnp.where(owner == o, both[0:1, 0:count], 0.0)
    scores_ref[...] = scores
    pose_ref[0:7, :] = total[1:8, 0:count]
    pose_ref[7:12, :] = pltpu.roll(total, 128 - count, 1)[0:5, 0:count]


def local(coords, atom_type, channel, charge, pair_owner, pair_slot, type_table, widths, tmpl_points, tmpl_weights):
    block_count, per_block = pair_owner.shape
    tmpl_count = tmpl_points.shape[0]
    owners = lax.axis_size(OWN)
    pair_count = block_count * per_block
    capacity = max(2, 2 * pair_count // owners)
    pts = tmpl_points.transpose(1, 0, 2).reshape(3 * tmpl_count, 128)
    wts = tmpl_weights.transpose(1, 0, 2).reshape(5 * tmpl_count, 128)
    templates = pl.pallas_call(
        template_kernel,
        out_shape=(
            jax.ShapeDtypeStruct(pts.shape, f32),
            jax.ShapeDtypeStruct(wts.shape, f32),
            jax.ShapeDtypeStruct((48 * tmpl_count, 128), bf16),
        ),
        compiler_params=pltpu.CompilerParams(vmem_limit_bytes=TEMPLATE_LIMIT),
        cost_estimate=pl.CostEstimate(flops=4000 * 128 * tmpl_count, bytes_accessed=8000 * tmpl_count, transcendentals=0),
        name="templates",
    )(pts, wts)

    if capacity >= block_count:
        rows = block_count // 2
        mine, consts = pl.pallas_call(
            functools.partial(pack_kernel, tmpl=tmpl_count),
            out_shape=(jax.ShapeDtypeStruct((PLANES * rows + 8, 128), f32), jax.ShapeDtypeStruct((8, 128), f32)),
            name="pack",
        )(coords.transpose(1, 0, 2), charge, atom_type, channel, pair_owner.T, pair_slot.T, widths[None], type_table.T)

        def shifted(x, axis, k):
            size = lax.axis_size(axis)
            return lax.ppermute(x, axis, [(i, (i + k) % size) for i in range(size)])

        tm_shifts = range(1, lax.axis_size("tmpl"))
        lib_shifts = range(1, lax.axis_size("lib"))
        beside = [shifted(mine, "tmpl", k) for k in tm_shifts]
        along = [shifted(mine, "lib", k) for k in lib_shifts]
        beside, along, templates = lax.optimization_barrier((beside, along, templates))
        along = jnp.stack(along)
        across = [shifted(along, "tmpl", k) for k in tm_shifts]
        near = jnp.concatenate([jnp.stack([mine] + beside), along])
        near = [near, shifted(near, "sub", 1)]
        chips = [(0, k) for k in (0, *tm_shifts)] + [(k, 0) for k in lib_shifts]
        shape = (2 * owners, 8, 128)
        done = pair_sums(near, consts, templates, chips, shape)
        across, done = lax.optimization_barrier((across, done))
        across = across[0] if len(across) == 1 else jnp.concatenate(across)
        across = [across, shifted(across, "sub", 1)]
        chips = [(k, q) for q in tm_shifts for k in lib_shifts]
        wg, out = pair_sums(across, consts, templates, chips, shape, done)
        got = lax.all_to_all(out, OWN + ("sub",), split_axis=0, concat_axis=0, tiled=True)
        scores, pose_grad = pl.pallas_call(
            merge_kernel,
            out_shape=(jax.ShapeDtypeStruct((per_block, block_count), f32), jax.ShapeDtypeStruct((12, block_count), f32)),
            name="merge",
        )(got, pair_owner.T)
        scores, pose_grad = scores.T, pose_grad.T
    else:
        consts = pl.pallas_call(const_rows, out_shape=jax.ShapeDtypeStruct((8, 128), f32), name="consts")(widths[None], type_table.T)
        tids = (pair_owner * tmpl_count + pair_slot).astype(f32)
        atoms = jnp.concatenate(
            [coords.transpose(1, 0, 2), jnp.stack([charge, atom_type.astype(f32), channel.astype(f32)])], axis=0
        )
        owner_ids = pair_owner.reshape(pair_count)
        order = jnp.arange(pair_count, dtype=i32)
        earlier = (owner_ids[None, :] == owner_ids[:, None]) & (order[None, :] < order[:, None])
        rank = jnp.sum(earlier.astype(i32), axis=1)
        place = owner_ids * capacity + rank
        slots = jnp.arange(owners * capacity, dtype=i32)
        selector = (slots[:, None] == place[None, :]).astype(f32)
        by_block = jnp.sum(selector.reshape(-1, block_count, per_block), axis=2)
        outgoing = jnp.einsum("sb,rbx->srx", by_block, atoms, precision=lax.Precision.HIGHEST)
        labels = jnp.sum(selector * (tids.reshape(pair_count)[None] + 1.0), axis=1) - 1.0
        labels = jnp.pad(labels[:, None], ((0, 0), (0, 127)), constant_values=-1.0)
        outgoing = jnp.concatenate([outgoing, labels[:, None]], axis=1)
        arrived = lax.all_to_all(outgoing, OWN, split_axis=0, concat_axis=0, tiled=True)
        groups = 16
        rows = owners * capacity // groups
        atoms = arrived[:, :PLANES].reshape(groups, rows, PLANES, 128).transpose(0, 2, 1, 3).reshape(groups, PLANES * rows, 128)
        ids = arrived[:, PLANES, 0].reshape(groups, 1, rows)
        ids = jnp.pad(ids, ((0, 0), (0, 7), (0, 128 - rows)), constant_values=-1.0)
        wg, res = pair_sums([jnp.concatenate([atoms, ids], axis=1)], consts, templates)
        res = lax.psum(res.T, "sub")
        got = lax.all_to_all(res, OWN, split_axis=0, concat_axis=0, tiled=True)
        per_pair = jnp.einsum("sp,sx->px", selector, got[:, :13], precision=lax.Precision.HIGHEST)
        scores = per_pair[:, 0].reshape(block_count, per_block)
        pose_grad = jnp.sum(per_pair[:, 1:].reshape(block_count, per_block, 12), axis=1)
    return scores, pose_grad, wg.reshape(5, tmpl_count, 128).transpose(1, 0, 2)


def solution(mesh):
    in_specs = (
        P(("groups", "lib", "tmpl"), None, None),
        P(("groups", "lib", "tmpl"), None),
        P(("groups", "lib", "tmpl"), None),
        P(("groups", "lib", "tmpl"), None),
        P(("groups", "lib", "tmpl"), None),
        P(("groups", "lib", "tmpl"), None),
        P(),
        P(),
        P(("lib", "tmpl"), None, "sub"),
        P(("lib", "tmpl"), None, "sub"),
    )
    out_specs = (
        P(("groups", "lib", "tmpl"), None),
        P(("groups", "lib", "tmpl"), None),
        P(("groups", "lib", "tmpl"), None, "sub"),
    )
    return jax.shard_map(local, mesh=mesh, in_specs=in_specs, out_specs=out_specs, check_vma=False)
```

```python
import functools
import math
import jax
import jax.numpy as jnp
from jax import lax
from jax.experimental import pallas as pl
from jax.experimental.pallas import tpu as pltpu
from jax.sharding import PartitionSpec as P

bf16, f32, i32 = jnp.bfloat16, jnp.float32, jnp.int32
LOG2E = math.log2(math.e)
OWN = ("lib", "tmpl")
PLANES = 6
SENDS = 2
VMEM_LIMIT = 36 * 1024 * 1024
TEMPLATE_LIMIT = 36 * 1024 * 1024


def split3(x):
    h = x.astype(bf16).astype(f32)
    r = x - h
    m = r.astype(bf16).astype(f32)
    return h, m, r - m


def split2(x):
    h = x.astype(bf16)
    return h, (x - h.astype(f32)).astype(bf16)


def iota(shape, axis):
    return lax.broadcasted_iota(i32, shape, axis)


def sum_lanes(m):
    h, l = split2(m)
    dims = (((1,), (1,)), ((), ()))
    o = lax.dot_general(jnp.ones((8, 256), bf16), jnp.concatenate([h, l], axis=1), dims, preferred_element_type=f32)
    return o[0:1]


def pair_kernel(*refs, lay):
    PP, UNROLL = lay.pairs, lay.unroll
    blocks, tmpl, rows, groups, srcs_n = lay.blocks, lay.tmpl, lay.rows, lay.groups, lay.arrays
    srcs, refs = refs[:srcs_n], refs[srcs_n:]
    prior, refs = (refs[:2], refs[2:]) if lay.prior else (None, refs)
    const_ref, pts_ref, v_ref, yk_ref, wg_out, out_ref = refs[:6]
    feats_ref, tids_ref, s_ref, res_ref, idv_ref, ids_ref, sem, idsem = refs[6:14]
    bufs = refs[14:]
    wg_ref, bufs = (bufs[0], bufs[1:]) if lay.last else (wg_out, bufs)
    half = len(bufs) // 2
    A, B = bufs[:half], bufs[half:]
    each = groups // srcs_n
    copies, id_copies = [], []
    for k, x in enumerate(srcs):
        at_ = pl.ds(k * each, each)
        id_copies.append(pltpu.make_async_copy(x.at[:, pl.ds(PLANES * rows, 8), :], tids_ref.at[at_], sem.at[k]))
        copies.append(pltpu.make_async_copy(x, feats_ref.at[at_], sem.at[srcs_n + k]))
    for c in id_copies + copies:
        c.start()
    for c in id_copies:
        c.wait()
    owner = lax.axis_index("lib") * lax.axis_size("tmpl") + lax.axis_index("tmpl")
    near = tids_ref[...] - (owner * tmpl).astype(f32)
    named = (near >= 0.0) & (near < float(tmpl)) & (iota(near.shape, 1) < 4)
    idv_ref[...] = jnp.max(jnp.where(named, near + 1.0, 0.0), axis=1).astype(i32) - 1
    copy = pltpu.make_async_copy(idv_ref, ids_ref, idsem)
    copy.start()
    wg_ref[...] = prior[0][...] if lay.prior else jnp.zeros_like(wg_ref)
    width = [jnp.broadcast_to(const_ref[f : f + 1, :], (8, 128)) for f in range(5)]
    force = [-2.0 * w for w in width]
    s0 = -LOG2E * width[0]
    ratio = (width[1] / width[0])[0:1]
    row8 = iota((8, 128), 0)
    lane8 = iota((8, 128), 1)
    by_chan = jnp.where(lane8 < 16, force[2], jnp.where(lane8 < 32, force[3], force[4]))
    top = row8 == 0
    tab0 = jnp.broadcast_to(const_ref[5:6, :], (8, 128)) * jnp.where(top, 1.0, force[0])
    tab1 = jnp.broadcast_to(const_ref[6:7, :], (8, 128)) * jnp.where(top, 1.0, by_chan)
    tabs = -LOG2E * jnp.where(lane8 == 0, width[2], jnp.where(lane8 == 1, width[3], width[4]))
    charge_scale = jnp.where(top, 1.0, force[1])
    chan_of_row = jnp.where((row8 > 0) & (row8 < 7), (row8 - 1) // 2, -1).astype(f32)

    copy.wait()
    for c in copies:
        c.wait()

    def slot(b0, u):
        g = lax.div(b0, rows)
        base = 0 if lay.dense else rows * lax.rem(lax.div(g, each) + lax.axis_index("sub"), 2)
        t = ids_ref[g, base + lax.rem(b0, rows) + u]
        return jnp.maximum(t, 0), t >= 0

    def stage0(b0, xt_ref, w_ref):
        for u in range(PP // 2):
            cols = []
            for k in range(2):
                _, valid = slot(b0, 2 * u + k)
                off = jnp.where(valid, 0.0, 64.0)

                def row(q):
                    at_ = q * rows + lax.rem(b0, rows) + 2 * u + k
                    return jnp.broadcast_to(feats_ref[lax.div(b0, rows), pl.ds(at_, 1), :], (8, 128))

                x0, x1, x2 = row(0), row(1), row(2)
                chan = row(5)
                kind = row(4) + off
                steric = jnp.take_along_axis(tab0, kind.astype(i32), axis=1)
                strength = jnp.take_along_axis(tab1, (kind + 16.0 * chan).astype(i32), axis=1)
                sph = jnp.take_along_axis(tabs, chan.astype(i32), axis=1)
                charge = row(3) * (charge_scale * valid.astype(f32))
                p = jnp.where((row8 == 1) | (row8 == 4) | (row8 == 7), x0, jnp.where((row8 == 2) | (row8 == 5), x1,
                    jnp.where((row8 == 3) | (row8 == 6), x2, 1.0)))
                q = jnp.where(row8 == 4, x0, jnp.where((row8 == 5) | (row8 == 7), x1, jnp.where(row8 == 6, x2, 1.0)))
                lo8 = p * q
                cross = jnp.where(lax.rem(row8, 2) == 1, x0, x1) * x2
                hi8 = jnp.where((row8 == 1) | (row8 == 2), cross, jnp.where(row8 == 7, 1.0, 0.0))
                parts_ = []
                for sc in (s0, sph):
                    h, m, l = split3(lo8 * sc)
                    parts_.append(jnp.concatenate([h, h, h, m, m, l], axis=0))
                cols.append(jnp.concatenate(parts_, axis=1))
                z = lo8 * strength
                zs = [jnp.where(chan == float(c), z, 0.0) for c in range(3)]
                zs.append(jnp.where(chan == chan_of_row, strength * cross, 0.0))
                ws = [[lo8 * steric, hi8 * steric], [lo8 * charge, hi8 * charge], zs]
                ws = [split2(jnp.concatenate(w, axis=0)) for w in ws]
                w_ref[2 * u + k] = jnp.concatenate([x for pair in ws for x in pair], axis=0)
            xt_ref[u] = jnp.concatenate(cols, axis=0).astype(bf16).T

    def stage1(b0, xt_ref, a_ref):
        for u in range(PP // 2):
            rhs = []
            for k in range(2):
                t, _ = slot(b0, 2 * u + k)
                yk = yk_ref[pl.ds(pl.multiple_of(t * 48, 16), 48), :]
                z = jnp.zeros_like(yk)
                rhs.append(jnp.concatenate([yk, z] if k == 0 else [z, yk], axis=1))
            a_ref[u] = jnp.dot(xt_ref[u], jnp.concatenate(rhs, axis=0), preferred_element_type=f32)

    def stage2(a_ref, w_ref, r_ref):
        for q in range(PP):
            js = slice(128 * (q % 2), 128 * (q % 2) + 128)

            def contract(e, at, n):
                eh, el = split2(e)
                w = w_ref[q, at : at + 2 * n]
                o = jnp.dot(jnp.concatenate([w, w], axis=1), jnp.concatenate([eh, el], axis=0), preferred_element_type=f32)
                return o[:n] + o[n:]

            a0 = a_ref[q // 2, 0:128, js]
            r_ref[q, 0:16] = contract(jnp.exp2(a0), 0, 16)
            r_ref[q, 16:32] = contract(jnp.exp2(a0 * ratio), 32, 16)
            r_ref[q, 32:64] = contract(jnp.exp2(a_ref[q // 2, 128:256, js]), 64, 32)

    def stage3(b0, r_ref):
        for q in range(PP):
            t, _ = slot(b0, q)
            b = b0 + q
            v = [jnp.broadcast_to(v_ref[pl.ds(f * tmpl + t, 1), :], (8, 128)) for f in range(5)]
            r = [r_ref[q, 8 * k : 8 * k + 8] for k in range(8)]
            z = [r[4 + c] * v[2 + c] for c in range(3)]
            lo = r[0] * v[0] + r[2] * v[1] + (z[0] + z[1] + z[2])
            t0 = z[0] * force[2] + z[1] * force[3] + z[2] * force[4]
            hi = r[1] * v[0] + r[3] * v[1] + r[7] * jnp.where(row8 < 3, v[2], jnp.where(row8 < 5, v[3], v[4]))
            for f, k in enumerate((0, 2, 4, 5, 6)):
                dst = pl.ds(f * tmpl + t, 1)
                wg_ref[dst, :] = wg_ref[dst, :] + r[k][0:1]
            rows_ = [lo[n : n + 1] for n in range(8)] + [t0[0:1]] + [hi[n : n + 1] for n in range(1, 8)]
            rows_ += [pts_ref[pl.ds(c * tmpl + t, 1), :] for c in range(3)]
            for n, x in enumerate(rows_):
                s_ref[pl.ds(n * blocks + b, 1), :] = x

    n = blocks // PP

    def halfstep(i, stages=(3, 2, 1, 0), even=None):
        src, dst = (A, B) if even else (B, A)
        xt_s, a_s, w_s, r_s = src
        xt_d, a_d, w_d, r_d = dst
        if 3 in stages:
            stage3((i - 3) * PP, r_s)
        if 2 in stages:
            stage2(a_s, w_d, r_d)
        if 1 in stages:
            stage1((i - 1) * PP, xt_s, a_d)
        if 0 in stages:
            stage0(i * PP, xt_d, w_d)

    def step(k, _):
        for u in range(UNROLL):
            halfstep(first + UNROLL * k + u, even=(first + u) % 2 == 0)
        return 0

    first = min(n, 3)
    while (n - first) % UNROLL or UNROLL % 2:
        first += 1
    for i in range(first):
        halfstep(i, [q for q in range(3, -1, -1) if i >= q], i % 2 == 0)
    if n > first:
        lax.fori_loop(0, (n - first) // UNROLL, step, 0)
    for i in range(n, n + 3):
        halfstep(i, [q for q in range(3, 0, -1) if i - q < n], i % 2 == 0)

    sends = []
    if lay.last:
        part = 5 * tmpl // SENDS
        for k in range(SENDS):
            at_ = pl.ds(k * part, part)
            sends.append(pltpu.make_async_copy(wg_ref.at[at_], wg_out.at[at_], sem.at[k]))
            sends[-1].start()

    def col(k):
        return s_ref[k * blocks : (k + 1) * blocks, :]

    y = [col(16 + c) for c in range(3)]
    xz, yz = col(9) + col(11) + col(13), col(10) + col(12) + col(14)
    second = [[col(4), col(7), xz], [col(7), col(5), yz], [xz, yz, col(6)]]
    t0 = col(8) + col(15)
    res_ref[...] = jnp.zeros_like(res_ref)
    res_ref[0:1, 0:blocks] = sum_lanes(col(0))
    for c in range(3):
        res_ref[1 + c : 2 + c, 0:blocks] = sum_lanes(col(1 + c) - y[c] * t0)
        for d in range(3):
            k = 4 + 3 * c + d
            res_ref[k : k + 1, 0:blocks] = sum_lanes(second[c][d] - y[c] * col(1 + d))
    if lay.dense:
        out_ref[...] = res_ref[:, 0:blocks]
        for c in sends:
            c.wait()
        return
    out_ref[...] = prior[1][...] if lay.prior else jnp.zeros_like(out_ref)
    lib, tm = lax.axis_index("lib"), lax.axis_index("tmpl")
    libs, tms = lax.axis_size("lib"), lax.axis_size("tmpl")
    for q, (up, over) in enumerate(lay.chips):
        piece = None
        for k in range(2):
            for h in range(2):
                start, to = (h * each + q) * rows, (2 * k + h) * rows
                x = res_ref[8 * k : 8 * k + 8, start // 128 * 128 : start // 128 * 128 + 128]
                shift = (to - start) % 128
                x = pltpu.roll(x, shift, 1) if shift else x
                piece = x if piece is None else jnp.where(lane8 < to, piece, x)
        chip = lax.rem(lib + libs - up, libs) * tms + lax.rem(tm + tms - over, tms)
        for s in range(2):
            out_ref[2 * chip + s] = piece
    for c in sends:
        c.wait()


class Layout:
    def __init__(self, feats, tmpl, chips, prior):
        self.arrays, self.tmpl, self.chips, self.prior = len(feats), tmpl, chips, prior
        self.last = prior or not chips
        self.dense = not chips
        self.groups = sum(x.shape[0] for x in feats)
        self.rows = (feats[0].shape[1] - 8) // PLANES
        self.blocks = self.groups * self.rows
        self.pairs, self.unroll = (16, 2) if self.blocks >= 128 else (8, 4)


def pair_sums(feats, consts, templates, chips=(), out=None, prior=None):
    lay = Layout(feats, templates[0].shape[0] // 3, chips, prior is not None)
    blocks, tmpl, groups, PP = lay.blocks, lay.tmpl, lay.groups, lay.pairs
    out = out or (16, blocks)
    hbm, vmem = (pl.BlockSpec(memory_space=m) for m in (pl.ANY, pltpu.VMEM))
    stages = [
        pltpu.VMEM((PP // 2, 256, 96), bf16),
        pltpu.VMEM((PP // 2, 256, 256), f32),
        pltpu.VMEM((PP, 128, 128), bf16),
        pltpu.VMEM((PP, 64, 128), f32),
    ]
    elements = blocks * 128 * 128
    return pl.pallas_call(
        functools.partial(pair_kernel, lay=lay),
        out_shape=(jax.ShapeDtypeStruct((5 * tmpl, 128), f32), jax.ShapeDtypeStruct(out, f32)),
        in_specs=[hbm] * len(feats) + [vmem] * (2 * lay.prior) + [vmem] * 4,
        out_specs=(hbm if lay.last else vmem, vmem),
        scratch_shapes=[
            pltpu.VMEM((groups,) + feats[0].shape[1:], f32),
            pltpu.VMEM((groups, 8, 128), f32),
            pltpu.VMEM((19 * blocks, 128), f32),
            pltpu.VMEM((16, -(-blocks // 128) * 128), f32),
            pltpu.VMEM((groups, 128), i32),
            pltpu.SMEM((groups, 128), i32),
            pltpu.SemaphoreType.DMA((max(SENDS, 2 * len(feats)),)),
            pltpu.SemaphoreType.DMA,
        ] + [pltpu.VMEM((5 * tmpl, 128), f32)] * lay.last + stages + stages,
        compiler_params=pltpu.CompilerParams(vmem_limit_bytes=VMEM_LIMIT),
        cost_estimate=pl.CostEstimate(flops=700 * elements, bytes_accessed=10 * elements // 8, transcendentals=3 * elements),
        name="gauss",
    )(*feats, *(prior or ()), consts, *templates)


def template_kernel(pts_ref, wts_ref, pts_out, v_ref, yk_ref):
    tmpl = pts_ref.shape[0] // 3
    pts_out[...] = pts_ref[...]
    v_ref[...] = wts_ref[...].astype(f32)
    row8 = iota((8, 128), 0)

    def step(i, _):
        for u in range(8):
            t = i * 8 + u
            y = [jnp.broadcast_to(pts_ref[pl.ds(c * tmpl + t, 1), :], (8, 128)) for c in range(3)]
            sq = y[0] * y[0] + y[1] * y[1] + y[2] * y[2]
            yf = jnp.where(row8 == 0, sq, jnp.where(row8 < 4, -2.0 * jnp.where(row8 == 1, y[0], jnp.where(row8 == 2, y[1], y[2])),
                 jnp.where(row8 < 7, 1.0, 0.0)))
            h, m, l = split3(yf)
            yk_ref[pl.ds(pl.multiple_of(t * 48, 16), 48), :] = jnp.concatenate([h, m, l, h, m, h], axis=0).astype(bf16)
        return 0

    lax.fori_loop(0, tmpl // 8, step, 0)


def const_rows(widths_ref, table_ref, const_ref):
    const_ref[...] = jnp.zeros_like(const_ref)
    kinds = table_ref.shape[1]
    for f in range(5):
        const_ref[f : f + 1, :] = jnp.broadcast_to(widths_ref[0:1, f : f + 1], (1, 128))
    const_ref[5:6, 0:kinds] = table_ref[0:1, :]
    for c in range(3):
        const_ref[6:7, kinds * c : kinds * (c + 1)] = table_ref[1:2, :]


def pack_kernel(xyz_ref, charge_ref, kind_ref, chan_ref, owner_ref, slot_ref, widths_ref, table_ref, out_ref, const_ref, *, tmpl):
    const_rows(widths_ref, table_ref, const_ref)
    rows = (out_ref.shape[0] - 8) // PLANES
    mine = pl.ds(pl.multiple_of(lax.axis_index("sub") * rows, rows), rows)
    planes = [xyz_ref[c, mine, :] for c in range(3)]
    planes += [charge_ref[mine, :], kind_ref[mine, :].astype(f32), chan_ref[mine, :].astype(f32)]
    top, count = owner_ref.shape
    for k, x in enumerate(planes):
        out_ref[k * rows : (k + 1) * rows, :] = x
    out_ref[PLANES * rows :, :] = jnp.full((8, 128), -1.0, f32)
    out_ref[PLANES * rows : PLANES * rows + top, 0:count] = (owner_ref[...] * tmpl + slot_ref[...]).astype(f32)


def merge_kernel(got_ref, owner_ref, scores_ref, pose_ref):
    top, count = owner_ref.shape
    rows = count // 2
    lane = iota((8, 128), 1)
    total = None
    owner = owner_ref[...]
    scores = jnp.zeros((top, count), f32)
    for o in range(got_ref.shape[0] // 2):
        other = got_ref[2 * o + 1]
        other = jnp.where(lax.rem(lane, count) < rows, pltpu.roll(other, 128 - rows, 1), pltpu.roll(other, rows, 1))
        both = got_ref[2 * o] + other
        total = both if total is None else total + both
        scores = scores + jnp.where(owner == o, both[0:1, 0:count], 0.0)
    scores_ref[...] = scores
    pose_ref[0:7, :] = total[1:8, 0:count]
    pose_ref[7:12, :] = pltpu.roll(total, 128 - count, 1)[0:5, 0:count]


def local(coords, atom_type, channel, charge, pair_owner, pair_slot, type_table, widths, tmpl_points, tmpl_weights):
    block_count, per_block = pair_owner.shape
    tmpl_count = tmpl_points.shape[0]
    owners = lax.axis_size(OWN)
    pair_count = block_count * per_block
    capacity = max(2, 2 * pair_count // owners)
    pts = tmpl_points.transpose(1, 0, 2).reshape(3 * tmpl_count, 128)
    wts = tmpl_weights.transpose(1, 0, 2).reshape(5 * tmpl_count, 128)
    templates = pl.pallas_call(
        template_kernel,
        out_shape=(
            jax.ShapeDtypeStruct(pts.shape, f32),
            jax.ShapeDtypeStruct(wts.shape, f32),
            jax.ShapeDtypeStruct((48 * tmpl_count, 128), bf16),
        ),
        compiler_params=pltpu.CompilerParams(vmem_limit_bytes=TEMPLATE_LIMIT),
        cost_estimate=pl.CostEstimate(flops=4000 * 128 * tmpl_count, bytes_accessed=8000 * tmpl_count, transcendentals=0),
        name="templates",
    )(pts, wts)

    if capacity >= block_count:
        rows = block_count // 2
        mine, consts = pl.pallas_call(
            functools.partial(pack_kernel, tmpl=tmpl_count),
            out_shape=(jax.ShapeDtypeStruct((PLANES * rows + 8, 128), f32), jax.ShapeDtypeStruct((8, 128), f32)),
            name="pack",
        )(coords.transpose(1, 0, 2), charge, atom_type, channel, pair_owner.T, pair_slot.T, widths[None], type_table.T)

        def shifted(x, axis, k):
            size = lax.axis_size(axis)
            return lax.ppermute(x, axis, [(i, (i + k) % size) for i in range(size)])

        tm_shifts = range(1, lax.axis_size("tmpl"))
        lib_shifts = range(1, lax.axis_size("lib"))
        beside = [shifted(mine, "tmpl", k) for k in tm_shifts]
        along = [shifted(mine, "lib", k) for k in lib_shifts]
        beside, along, templates = lax.optimization_barrier((beside, along, templates))
        along = jnp.stack(along)
        across = [shifted(along, "tmpl", k) for k in tm_shifts]
        near = jnp.concatenate([jnp.stack([mine] + beside), along])
        near = [near, shifted(near, "sub", 1)]
        chips = [(0, k) for k in (0, *tm_shifts)] + [(k, 0) for k in lib_shifts]
        shape = (2 * owners, 8, 128)
        done = pair_sums(near, consts, templates, chips, shape)
        across, done = lax.optimization_barrier((across, done))
        across = across[0] if len(across) == 1 else jnp.concatenate(across)
        across = [across, shifted(across, "sub", 1)]
        chips = [(k, q) for q in tm_shifts for k in lib_shifts]
        wg, out = pair_sums(across, consts, templates, chips, shape, done)
        got = lax.all_to_all(out, OWN + ("sub",), split_axis=0, concat_axis=0, tiled=True)
        scores, pose_grad = pl.pallas_call(
            merge_kernel,
            out_shape=(jax.ShapeDtypeStruct((per_block, block_count), f32), jax.ShapeDtypeStruct((12, block_count), f32)),
            name="merge",
        )(got, pair_owner.T)
        scores, pose_grad = scores.T, pose_grad.T
    else:
        consts = pl.pallas_call(const_rows, out_shape=jax.ShapeDtypeStruct((8, 128), f32), name="consts")(widths[None], type_table.T)
        tids = (pair_owner * tmpl_count + pair_slot).astype(f32)
        atoms = jnp.concatenate(
            [coords.transpose(1, 0, 2), jnp.stack([charge, atom_type.astype(f32), channel.astype(f32)])], axis=0
        )
        owner_ids = pair_owner.reshape(pair_count)
        order = jnp.arange(pair_count, dtype=i32)
        earlier = (owner_ids[None, :] == owner_ids[:, None]) & (order[None, :] < order[:, None])
        rank = jnp.sum(earlier.astype(i32), axis=1)
        place = owner_ids * capacity + rank
        slots = jnp.arange(owners * capacity, dtype=i32)
        selector = (slots[:, None] == place[None, :]).astype(f32)
        by_block = jnp.sum(selector.reshape(-1, block_count, per_block), axis=2)
        outgoing = jnp.einsum("sb,rbx->srx", by_block, atoms, precision=lax.Precision.HIGHEST)
        labels = jnp.sum(selector * (tids.reshape(pair_count)[None] + 1.0), axis=1) - 1.0
        labels = jnp.pad(labels[:, None], ((0, 0), (0, 127)), constant_values=-1.0)
        outgoing = jnp.concatenate([outgoing, labels[:, None]], axis=1)
        arrived = lax.all_to_all(outgoing, OWN, split_axis=0, concat_axis=0, tiled=True)
        groups = 16
        rows = owners * capacity // groups
        atoms = arrived[:, :PLANES].reshape(groups, rows, PLANES, 128).transpose(0, 2, 1, 3).reshape(groups, PLANES * rows, 128)
        ids = arrived[:, PLANES, 0].reshape(groups, 1, rows)
        ids = jnp.pad(ids, ((0, 0), (0, 7), (0, 128 - rows)), constant_values=-1.0)
        wg, res = pair_sums([jnp.concatenate([atoms, ids], axis=1)], consts, templates)
        res = lax.psum(res.T, "sub")
        got = lax.all_to_all(res, OWN, split_axis=0, concat_axis=0, tiled=True)
        per_pair = jnp.einsum("sp,sx->px", selector, got[:, :13], precision=lax.Precision.HIGHEST)
        scores = per_pair[:, 0].reshape(block_count, per_block)
        pose_grad = jnp.sum(per_pair[:, 1:].reshape(block_count, per_block, 12), axis=1)
    return scores, pose_grad, wg.reshape(5, tmpl_count, 128).transpose(1, 0, 2)


def solution(mesh):
    in_specs = (
        P(("groups", "lib", "tmpl"), None, None),
        P(("groups", "lib", "tmpl"), None),
        P(("groups", "lib", "tmpl"), None),
        P(("groups", "lib", "tmpl"), None),
        P(("groups", "lib", "tmpl"), None),
        P(("groups", "lib", "tmpl"), None),
        P(),
        P(),
        P(("lib", "tmpl"), None, "sub"),
        P(("lib", "tmpl"), None, "sub"),
    )
    out_specs = (
        P(("groups", "lib", "tmpl"), None),
        P(("groups", "lib", "tmpl"), None),
        P(("groups", "lib", "tmpl"), None, "sub"),
    )
    return jax.shard_map(local, mesh=mesh, in_specs=in_specs, out_specs=out_specs, check_vma=False)
```
